128 devices in a mesh: rep: 4 (over y), row: 32 (over x, z, core).
Axes of the slice: x: 4, y: 4, z: 4, core: 2. Of those that a mesh axis runs over, the one named last changes fastest.
Arguments:
- grads: bfloat16 [4, 2, 6144, 8192], P('rep', None, 'row'), may hold values from -6 to 6
- errors: bfloat16 [4, 2, 6144, 8192], P('rep', None, 'row'), may hold values from -4 to 4
- q_init: float32 [2, 32, 8192], replicated, may hold values from -0.0625 to 0.0625
Outputs:
- new_errors: bfloat16 [4, 2, 6144, 8192], P('rep', None, 'row')
- q_new: float32 [2, 32, 8192], replicated
The draws below stay inside these ranges and needn't reach their ends.
All inputs are finite; a program needn't handle non-finite values.
Results may differ from the reference program's by a relative error of at most 0.001.
Values sent between devices are 32-bit elements; how exact they have to be, the bound alone decides.
A program may use at most 128 MiB of HBM per device.

```python
import jax
import jax.numpy as jnp
from jax import lax

D = 6144
FF = 8192
R = 32
EXP = 2
REPS = 4


def steps_of(stream_key, shape, split, low, high):
    level, own = 1.0, jax.random.fold_in(stream_key, 6)
    for dim, blocks in split:
        heights = jnp.exp(jax.random.uniform(jax.random.fold_in(own, dim), (blocks,), jnp.float32, low / len(split), high / len(split)))
        level = level * jnp.repeat(heights, shape[dim] // blocks).reshape([-1 if axis == dim else 1 for axis in range(len(shape))])
    return level


def gaussian(key, extent, deviation, limit, pieces=(), kind=jnp.bfloat16):
    gain = steps_of(key, extent, pieces, -0.22, 0.18) if pieces else 1.0
    array = jax.random.normal(key, extent, jnp.float32) * deviation * gain
    return jnp.minimum(jnp.maximum(array, -limit), limit).astype(kind)


def setup_inputs(seed: int = 0) -> dict:
    arg_keys = jax.random.split(jax.random.key(seed), 4)
    return {
        "grads": gaussian(arg_keys[0], (REPS, EXP, D, FF), 1.0, 6.0, ((0, 4), (2, 32))),
        "errors": gaussian(arg_keys[1], (REPS, EXP, D, FF), 0.5, 4.0, ((0, 4), (2, 32))),
        "q_init": gaussian(arg_keys[2], (EXP, R, FF), FF ** -0.5, 0.0625, (), jnp.float32),
    }


def reference(grads, errors, q_init):
    high = lax.Precision.HIGHEST
    error_list = []
    coeff_list = []
    for expert in range(EXP):
        panel = jnp.zeros((D, R), jnp.float32)
        for replica in range(REPS):
            merged = grads[replica, expert].astype(jnp.float32) + errors[replica, expert].astype(jnp.float32)
            panel = panel + jnp.dot(merged, q_init[expert].T, precision=high)
        panel = panel / REPS
        gram_total = jnp.dot(panel.T, panel, precision=high)
        factor = jnp.linalg.cholesky(gram_total)
        inverse = lax.linalg.triangular_solve(factor, jnp.eye(R, dtype=jnp.float32), left_side=True, lower=True)
        basis = jnp.dot(panel, inverse.T, precision=high)
        coeffs = jnp.zeros((R, FF), jnp.float32)
        for replica in range(REPS):
            merged = grads[replica, expert].astype(jnp.float32) + errors[replica, expert].astype(jnp.float32)
            coeffs = coeffs + jnp.dot(basis.T, merged, precision=high)
        coeffs = coeffs / REPS
        coeff_list.append(coeffs)
        per_replica = []
        for replica in range(REPS):
            merged = grads[replica, expert].astype(jnp.float32) + errors[replica, expert].astype(jnp.float32)
            per_replica.append((merged - jnp.dot(basis, coeffs, precision=high)).astype(jnp.bfloat16))
        error_list.append(jnp.stack(per_replica))
    new_errors = jnp.stack(error_list, axis=1)
    return (new_errors, jnp.stack(coeff_list))
```

```python
import jax
import jax.numpy as jnp
from jax import lax
from jax.experimental import pallas as pl
from jax.experimental.pallas import tpu as pltpu
from jax.sharding import PartitionSpec as P

EXP, ROWS, FF, R = 2, 192, 8192, 32
REPS, SIDE = 4, 4
UNITS = 4
UNIT = FF // UNITS
PIECE = UNIT // SIDE
TILE = PIECE // SIDE
MESH = pl.DeviceIdType.MESH
HIGH = lax.Precision.HIGHEST
NN = (((1,), (0,)), ((), ()))
NT = (((1,), (1,)), ((), ()))


def split(value, pieces):
    out = []
    for _ in range(pieces):
        piece = value.astype(jnp.bfloat16)
        out.append(piece)
        value = value - piece.astype(jnp.float32)
    return out


def dot(a, b, dims=NN):
    return lax.dot_general(a, b, dims, preferred_element_type=jnp.float32)


def dot_high(a, b, dims=NN):
    return lax.dot_general(a, b, dims, precision=HIGH, preferred_element_type=jnp.float32)


def kernel(
    g_hbm, e_hbm, q_hbm, fresh, coeffs,
    g, e, q, panels, left, basis, gram1, gram2, aug_ref, part, partner, r1, s2, r2, t3, full,
    load_sem, ps, pr, g1s, g1r, g2s, g2r, cs, cr, s1s, s1r, s2s, s2r, s3s, s3r, a2s, a2r, a1s, a1r, fs, fr,
):
    y = lax.axis_index("rep")
    row = lax.axis_index("row")
    c = lax.rem(row, 2)
    z = lax.rem(row // 2, SIDE)
    x = row // (2 * SIDE)
    me = (x, y, z)

    def at(place, core):
        return (place[1], place[0] * (2 * SIDE) + place[2] * 2 + core)

    def along(axis, d):
        return at([lax.rem(p + d * w, SIDE) for p, w in zip(me, axis)], c)

    def my(axis):
        return x * axis[0] + y * axis[1] + z * axis[2]

    ax, ay, az = (1, 0, 0), (0, 1, 0), (0, 0, 1)
    n = 1 - c
    orders = [(ax, ay, az), (ay, az, ax), (az, ax, ay), ((n, c, 0), (0, n, c), (c, 0, n))]
    other = at(me, 1 - c)

    def remote(src, dst, send, recv, device):
        return pltpu.make_async_remote_copy(
            src_ref=src, dst_ref=dst, send_sem=send, recv_sem=recv, device_id=device, device_id_type=MESH
        )

    loads = []
    for ex in range(EXP):
        for u in range(UNITS):
            cols = pl.ds(u * UNIT, UNIT)
            group = [
                pltpu.make_async_copy(q_hbm.at[ex, :, cols], q.at[ex, :, cols], load_sem.at[0, ex, u]),
                pltpu.make_async_copy(g_hbm.at[0, ex, :, cols], g.at[ex, :, cols], load_sem.at[1, ex, u]),
                pltpu.make_async_copy(e_hbm.at[0, ex, :, cols], e.at[ex, :, cols], load_sem.at[2, ex, u]),
            ]
            for copy in group:
                copy.start()
            loads.append(group)

    barrier = pltpu.get_barrier_semaphore()
    greeted = [along(axis, d) for axis in (ax, ay, az) for d in (1, 2, 3)]
    greeted += [at((lax.rem(x + d, SIDE), y, z), 1 - c) for d in range(SIDE)]
    for device in greeted:
        pl.semaphore_signal(barrier, inc=1, device_id=device, device_id_type=MESH)

    sends = []
    panel_recvs = []
    for ex in range(EXP):
        total = jnp.zeros((ROWS, 3 * R), jnp.float32)
        for u in range(UNITS):
            for copy in loads[ex * UNITS + u]:
                copy.wait()
            cols = pl.ds(u * UNIT, UNIT)
            q3 = jnp.concatenate(split(q[ex, :, cols], 3), axis=0)
            total += dot(g[ex, :, cols], q3, NT)
            total += dot(e[ex, :, cols], q3, NT)
        flat = jnp.concatenate([total, jnp.zeros((ROWS, R), jnp.float32)], axis=1).T
        panels[ex, y] = flat[0:R] + flat[R : 2 * R] + flat[2 * R : 3 * R]
        if ex == 0:
            pl.semaphore_wait(barrier, len(greeted))
        recvs = []
        for d in (1, 2, 3):
            copy = remote(panels.at[ex, y], panels.at[ex, y], ps.at[ex, d - 1], pr.at[ex, d - 1], along(ay, d))
            copy.start()
            sends.append(copy)
            recvs.append(copy)
        panel_recvs.append(recvs)

    def finish_panel(ex):
        for copy in panel_recvs[ex]:
            copy.wait_recv()
        panel = (panels[ex, 0] + panels[ex, 1] + panels[ex, 2] + panels[ex, 3]) * (1.0 / REPS)
        left[ex] = jnp.concatenate(split(panel, 3), axis=0)
        return panel

    def product(ex, u):
        def body(p, _):
            cols = pl.ds(pl.multiple_of(u * UNIT + p * PIECE, PIECE), PIECE)
            lhs = left[ex]
            both = dot(lhs, g[ex, :, cols]) + dot(lhs, e[ex, :, cols])
            part[ex, u, p] = both[0:R] + both[R : 2 * R] + both[2 * R : 3 * R]
            return 0

        lax.fori_loop(0, SIDE, body, 0)

    def to_partner(ex, u):
        return remote(part.at[ex, u], partner.at[u], cs.at[u], cr.at[u], other)

    def scatter1(ex, u, d):
        axis = orders[u][0]
        p = lax.rem(my(axis) + d, SIDE)
        return remote(part.at[ex, u, p], r1.at[u, d - 1], s1s.at[u, d - 1], s1r.at[u, d - 1], along(axis, d))

    def own_unit(ex, u):
        to_partner(ex, u).wait_recv()
        for p in range(SIDE):
            part[ex, u, p] = part[ex, u, p] + partner[u, p]
        for d in (1, 2, 3):
            scatter1(ex, u, d).start()

    def coefficients(ex):
        for u in range(UNITS):
            product(ex, u)

            @pl.when(c != ex)
            def _():
                to_partner(ex, u).start()

            if u > 0:

                @pl.when(c == ex)
                def _():
                    own_unit(ex, u - 1)

        @pl.when(c == ex)
        def _():
            own_unit(ex, UNITS - 1)

    panel0 = finish_panel(0)
    coefficients(0)
    panel1 = finish_panel(1)

    zeros = jnp.zeros((R, ROWS), jnp.float32)
    pad0 = jnp.concatenate([panel0, zeros, zeros, zeros], axis=0)
    pad1 = jnp.concatenate([zeros, zeros, panel1, zeros], axis=0)
    gram1[2 * x + c] = dot_high(panel0, pad0, NT) + dot_high(panel1, pad1, NT)
    gram1_copies = []
    for i in range(7):
        if i < 3:
            device = along(ax, i + 1)
        else:
            device = at((lax.rem(x + i - 3, SIDE), y, z), 1 - c)
        copy = remote(gram1.at[2 * x + c], gram1.at[2 * x + c], g1s.at[i], g1r.at[i], device)
        copy.start()
        gram1_copies.append(copy)

    coefficients(1)

    for copy in gram1_copies:
        copy.wait_recv()
    total = gram1[0]
    for i in range(1, 2 * SIDE):
        total += gram1[i]
    gram2[z] = total
    gram2_copies = []
    for d in (1, 2, 3):
        copy = remote(gram2.at[z], gram2.at[z], g2s.at[d - 1], g2r.at[d - 1], along(az, d))
        copy.start()
        gram2_copies.append(copy)

    def scatter2(u, d):
        axis = orders[u][1]
        p = lax.rem(my(axis) + d, SIDE)
        return remote(s2.at[u, p], r2.at[u, d - 1], s2s.at[u, d - 1], s2r.at[u, d - 1], along(axis, d))

    def scatter3(u, d):
        axis = orders[u][2]
        i = my(axis)
        return remote(t3.at[u, i], t3.at[u, i], s3s.at[u, d - 1], s3r.at[u, d - 1], along(axis, d))

    for u in range(UNITS):
        for d in (1, 2, 3):
            scatter1(c, u, d).wait_recv()
        mine = part[c, u, my(orders[u][0])] + r1[u, 0] + r1[u, 1] + r1[u, 2]
        for p in range(SIDE):
            s2[u, p] = mine[:, p * TILE : (p + 1) * TILE]
        for d in (1, 2, 3):
            scatter2(u, d).start()

    for copy in gram2_copies:
        copy.wait_recv()
    aug = gram2[0] + gram2[1] + gram2[2] + gram2[3]
    rows_at = lax.broadcasted_iota(jnp.int32, (R, 4 * R), 0)
    lanes_at = lax.broadcasted_iota(jnp.int32, (R, 4 * R), 1)
    unit_at = (lanes_at == rows_at + R) | (lanes_at == rows_at + 3 * R)
    aug = jnp.where(unit_at, 1.0, aug)
    first = lanes_at < 2 * R
    pivots = jnp.ones((R, 4 * R), jnp.float32)
    for k in range(R):
        column = jnp.where(first, aug[:, k : k + 1], aug[:, 2 * R + k : 2 * R + k + 1])
        pivot = column[k : k + 1, :]
        ratio = aug[k : k + 1, :] / pivot
        pivots = jnp.where(rows_at == k, pivot, pivots)
        aug = jnp.where(rows_at > k, aug - column * ratio, aug)
    aug = aug / jnp.sqrt(pivots)
    inverses = []
    for ex in range(EXP):
        wanted = (lanes_at >= (2 * ex + 1) * R) & (lanes_at < (2 * ex + 2) * R)
        inverses.append(jnp.where(wanted, aug, 0.0))
    aug_ref[0] = inverses[0]
    aug_ref[1] = inverses[1]

    for u in range(UNITS):
        for d in (1, 2, 3):
            scatter2(u, d).wait_recv()
        t3[u, my(orders[u][2])] = s2[u, my(orders[u][1])] + r2[u, 0] + r2[u, 1] + r2[u, 2]
        for d in (1, 2, 3):
            scatter3(u, d).start()

    for ex, panel in ((0, panel0), (1, panel1)):
        b = dot_high(inverses[ex], jnp.concatenate([panel] * 4, axis=0))
        hi, lo = [piece.astype(jnp.float32) for piece in split(b, 2)]
        basis[ex] = jnp.concatenate([hi, hi, lo, lo], axis=0).T.astype(jnp.bfloat16)

    def place(u):
        return c, u, my(orders[u][0]), my(orders[u][1])

    def gather2(u, d):
        spot = full.at[place(u)]
        return remote(spot, spot, a2s.at[u, d - 1], a2r.at[u, d - 1], along(orders[u][1], d))

    def gather1(u, d):
        spot = full.at[c, u, my(orders[u][0])]
        return remote(spot, spot, a1s.at[u, d - 1], a1r.at[u, d - 1], along(orders[u][0], d))

    def forward(u):
        return remote(full.at[c, u], full.at[c, u], fs.at[u], fr.at[u], other)

    for u in range(UNITS):
        for d in (1, 2, 3):
            scatter3(u, d).wait_recv()
        tile = t3[u, 0] + t3[u, 1] + t3[u, 2] + t3[u, 3]
        full[place(u)] = dot_high(aug_ref[c], jnp.concatenate([tile] * 4, axis=0)) * (1.0 / REPS)
        for d in (1, 2, 3):
            gather2(u, d).start()
    for u in range(UNITS):
        for d in (1, 2, 3):
            gather2(u, d).wait_recv()
        for d in (1, 2, 3):
            gather1(u, d).start()

    def residual(ex, u):
        def body(p, _):
            cols = pl.ds(pl.multiple_of(u * UNIT + p * PIECE, PIECE), PIECE)
            new = jnp.concatenate([full[ex, u, p, i] for i in range(SIDE)], axis=1)
            coeffs[ex, :, cols] = new
            hi, lo = split(new, 2)
            low = dot(basis[ex], jnp.concatenate([hi, lo, hi, lo], axis=0))
            merged = g[ex, :, cols].astype(jnp.float32) + e[ex, :, cols].astype(jnp.float32)
            fresh[0, ex, :, cols] = (merged - low).astype(jnp.bfloat16)
            return 0

        lax.fori_loop(0, SIDE, body, 0)

    for u in range(UNITS):
        for d in (1, 2, 3):
            gather1(u, d).wait_recv()
        forward(u).start()
        residual(c, u)
    for u in range(UNITS):
        forward(u).wait_recv()
        residual(1 - c, u)

    for copy in sends + gram1_copies + gram2_copies:
        copy.wait_send()
    for u in range(UNITS):
        to_partner(1 - c, u).wait_send()
        forward(u).wait_send()
        for d in (1, 2, 3):
            for copy in (scatter1(c, u, d), scatter2(u, d), scatter3(u, d), gather2(u, d), gather1(u, d)):
                copy.wait_send()


def shards(grads, errors, q_init):
    dma = pltpu.SemaphoreType.DMA
    anywhere = pl.BlockSpec(memory_space=pl.ANY)
    vmem = pl.BlockSpec(memory_space=pltpu.VMEM)
    f32, b16 = jnp.float32, jnp.bfloat16
    return pl.pallas_call(
        kernel,
        out_shape=(
            jax.ShapeDtypeStruct((1, EXP, ROWS, FF), b16),
            jax.ShapeDtypeStruct((EXP, R, FF), f32),
        ),
        in_specs=[anywhere] * 3,
        out_specs=(vmem, vmem),
        scratch_shapes=[
            pltpu.VMEM((EXP, ROWS, FF), b16),
            pltpu.VMEM((EXP, ROWS, FF), b16),
            pltpu.VMEM((EXP, R, FF), f32),
            pltpu.VMEM((EXP, REPS, R, ROWS), f32),
            pltpu.VMEM((EXP, 3 * R, ROWS), b16),
            pltpu.VMEM((EXP, ROWS, 4 * R), b16),
            pltpu.VMEM((2 * SIDE, R, 4 * R), f32),
            pltpu.VMEM((SIDE, R, 4 * R), f32),
            pltpu.VMEM((EXP, R, 4 * R), f32),
            pltpu.VMEM((EXP, UNITS, SIDE, R, PIECE), f32),
            pltpu.VMEM((UNITS, SIDE, R, PIECE), f32),
            pltpu.VMEM((UNITS, SIDE - 1, R, PIECE), f32),
            pltpu.VMEM((UNITS, SIDE, R, TILE), f32),
            pltpu.VMEM((UNITS, SIDE - 1, R, TILE), f32),
            pltpu.VMEM((UNITS, SIDE, R, TILE), f32),
            pltpu.VMEM((EXP, UNITS, SIDE, SIDE, R, TILE), f32),
            dma((3, EXP, UNITS)),
            dma((EXP, 3)), dma((EXP, 3)),
            dma((7,)), dma((7,)), dma((3,)), dma((3,)),
            dma((UNITS,)), dma((UNITS,)),
            dma((UNITS, 3)), dma((UNITS, 3)),
            dma((UNITS, 3)), dma((UNITS, 3)),
            dma((UNITS, 3)), dma((UNITS, 3)),
            dma((UNITS, 3)), dma((UNITS, 3)),
            dma((UNITS, 3)), dma((UNITS, 3)),
            dma((UNITS,)), dma((UNITS,)),
        ],
        compiler_params=pltpu.CompilerParams(
            collective_id=0, has_side_effects=True, vmem_limit_bytes=56 * 2**20
        ),
        cost_estimate=pl.CostEstimate(flops=10**9, bytes_accessed=25 * 10**6, transcendentals=0),
        name="compress",
    )(grads, errors, q_init)


def solution(mesh):
    in_specs = (P("rep", None, "row", None), P("rep", None, "row", None), P())
    out_specs = (P("rep", None, "row", None), P())
    return jax.shard_map(shards, mesh=mesh, in_specs=in_specs, out_specs=out_specs, check_vma=False)
```

```python
import jax
import jax.numpy as jnp
from jax import lax
from jax.experimental import pallas as pl
from jax.experimental.pallas import tpu as pltpu
from jax.sharding import PartitionSpec as P

EXP, ROWS, FF, R = 2, 192, 8192, 32
REPS, SIDE = 4, 4
UNITS = 4
UNIT = FF // UNITS
PIECE = UNIT // SIDE
TILE = PIECE // SIDE
LANES = 128
LOADS = 2
LOAD = FF // LOADS
MESH = pl.DeviceIdType.MESH
HIGH = lax.Precision.HIGHEST
NN = (((1,), (0,)), ((), ()))
NT = (((1,), (1,)), ((), ()))


def split(value, pieces):
    out = []
    for _ in range(pieces):
        piece = value.astype(jnp.bfloat16)
        out.append(piece)
        value = value - piece.astype(jnp.float32)
    return out


def dot(a, b, dims=NN):
    return lax.dot_general(a, b, dims, preferred_element_type=jnp.float32)


def dot_high(a, b, dims=NN):
    return lax.dot_general(a, b, dims, precision=HIGH, preferred_element_type=jnp.float32)


def kernel(
    g_hbm, e_hbm, q_hbm, fresh, coeffs,
    g, e, q, panels, left, basis, gram1, gram2, aug_ref, part, partner, r1, s2, r2, t3, full,
    load_sem, ps, pr, g1s, g1r, g2s, g2r, cs, cr, s1s, s1r, s2s, s2r, s3s, s3r, a2s, a2r, a1s, a1r, fs, fr,
):
    y = lax.axis_index("rep")
    row = lax.axis_index("row")
    c = lax.rem(row, 2)
    z = lax.rem(row // 2, SIDE)
    x = row // (2 * SIDE)
    me = (x, y, z)

    def at(place, core):
        return (place[1], place[0] * (2 * SIDE) + place[2] * 2 + core)

    def along(axis, d):
        return at([lax.rem(p + d * w, SIDE) for p, w in zip(me, axis)], c)

    def my(axis):
        return x * axis[0] + y * axis[1] + z * axis[2]

    ax, ay, az = (1, 0, 0), (0, 1, 0), (0, 0, 1)
    n = 1 - c
    orders = [(ax, ay, az), (ay, az, ax), (az, ax, ay), ((n, c, 0), (0, n, c), (c, 0, n))]
    other = at(me, 1 - c)

    def remote(src, dst, send, recv, device):
        return pltpu.make_async_remote_copy(
            src_ref=src, dst_ref=dst, send_sem=send, recv_sem=recv, device_id=device, device_id_type=MESH
        )

    def loads(ex, h):
        cols = pl.ds(pl.multiple_of(h * LOAD, LOAD), LOAD)
        return [
            pltpu.make_async_copy(q_hbm.at[ex, :, cols], q.at[ex, :, cols], load_sem.at[0, ex, h]),
            pltpu.make_async_copy(g_hbm.at[0, ex, :, cols], g.at[ex, :, cols], load_sem.at[1, ex, h]),
            pltpu.make_async_copy(e_hbm.at[0, ex, :, cols], e.at[ex, :, cols], load_sem.at[2, ex, h]),
        ]

    for ex in range(EXP):
        for h in range(LOADS):
            for copy in loads(ex, h):
                copy.start()

    barrier = pltpu.get_barrier_semaphore()
    greeted = [along(axis, d) for axis in (ax, ay, az) for d in (1, 2, 3)]
    greeted += [at((lax.rem(x + d, SIDE), y, z), 1 - c) for d in range(SIDE)]
    for device in greeted:
        pl.semaphore_signal(barrier, inc=1, device_id=device, device_id_type=MESH)

    def to_replica(ex, d):
        spot = panels.at[ex, y]
        return remote(spot, spot, ps.at[ex, d - 1], pr.at[ex, d - 1], along(ay, d))

    def panel_term(ex, _):
        def add(h, total):
            for copy in loads(ex, h):
                copy.wait()
            cols = pl.ds(pl.multiple_of(h * LOAD, LOAD), LOAD)
            q3 = jnp.concatenate(split(q[ex, :, cols], 3), axis=0)
            return total + (dot(g[ex, :, cols], q3, NT) + dot(e[ex, :, cols], q3, NT))

        total = lax.fori_loop(0, LOADS, add, jnp.zeros((ROWS, 3 * R), jnp.float32))
        flat = jnp.concatenate([total, jnp.zeros((ROWS, R), jnp.float32)], axis=1).T
        term = flat[0:R] + flat[R : 2 * R] + flat[2 * R : 3 * R]
        panels[ex, y, 0:R] = term[:, 0:LANES]
        panels[ex, y, R:] = jnp.concatenate([term[: R // 2, LANES:], term[R // 2 :, LANES:]], axis=1)

        @pl.when(ex == 0)
        def _():
            pl.semaphore_wait(barrier, len(greeted))

        for d in (2, 1, 3):
            to_replica(ex, d).start()
        return 0

    lax.fori_loop(0, EXP, panel_term, 0)

    def finish_panel(ex):
        for d in (1, 2, 3):
            to_replica(ex, d).wait_recv()
        packed = (panels[ex, 0] + panels[ex, 1] + panels[ex, 2] + panels[ex, 3]) * (1.0 / REPS)
        rest = packed[R:]
        rest = jnp.concatenate([rest[:, : LANES // 2], rest[:, LANES // 2 :]], axis=0)
        panel = jnp.concatenate([packed[0:R], rest], axis=1)
        left[ex] = jnp.concatenate(split(panel, 3), axis=0)
        return panel

    def product(ex, u):
        lhs = left[ex]
        for p in range(SIDE):
            cols = pl.ds(u * UNIT + p * PIECE, PIECE)
            both = dot(lhs, g[ex, :, cols]) + dot(lhs, e[ex, :, cols])
            part[ex, u, p] = both[0:R] + both[R : 2 * R] + both[2 * R : 3 * R]

    def to_partner(ex, u):
        return remote(part.at[ex, u], partner.at[u], cs.at[u], cr.at[u], other)

    def scatter1(ex, u, d):
        axis = orders[u][0]
        p = lax.rem(my(axis) + d, SIDE)
        return remote(part.at[ex, u, p], r1.at[u, d - 1], s1s.at[u, d - 1], s1r.at[u, d - 1], along(axis, d))

    def own_unit(ex, u):
        to_partner(ex, u).wait_recv()
        for p in range(SIDE):
            part[ex, u, p] = part[ex, u, p] + partner[u, p]
        for d in (2, 1, 3):
            scatter1(ex, u, d).start()

    def coefficients(ex):
        for u in range(UNITS):
            product(ex, u)

            @pl.when(c != ex)
            def _():
                to_partner(ex, u).start()

            if u > 0:

                @pl.when(c == ex)
                def _():
                    own_unit(ex, u - 1)

        @pl.when(c == ex)
        def _():
            own_unit(ex, UNITS - 1)

    panel0 = finish_panel(0)
    coefficients(0)
    panel1 = finish_panel(1)

    zeros = jnp.zeros((R, ROWS), jnp.float32)
    pad0 = jnp.concatenate([panel0, zeros, zeros, zeros], axis=0)
    pad1 = jnp.concatenate([zeros, zeros, panel1, zeros], axis=0)
    gram1[2 * x + c] = dot_high(panel0, pad0, NT) + dot_high(panel1, pad1, NT)
    gram1_copies = []
    for i in range(7):
        if i < 3:
            device = along(ax, i + 1)
        else:
            device = at((lax.rem(x + i - 3, SIDE), y, z), 1 - c)
        copy = remote(gram1.at[2 * x + c], gram1.at[2 * x + c], g1s.at[i], g1r.at[i], device)
        copy.start()
        gram1_copies.append(copy)

    coefficients(1)

    for copy in gram1_copies:
        copy.wait_recv()
    total = gram1[0]
    for i in range(1, 2 * SIDE):
        total += gram1[i]
    gram2[z] = total
    gram2_copies = []
    for d in (1, 2, 3):
        copy = remote(gram2.at[z], gram2.at[z], g2s.at[d - 1], g2r.at[d - 1], along(az, d))
        copy.start()
        gram2_copies.append(copy)

    def scatter2(u, d):
        axis = orders[u][1]
        p = lax.rem(my(axis) + d, SIDE)
        return remote(s2.at[u, p], r2.at[u, d - 1], s2s.at[u, d - 1], s2r.at[u, d - 1], along(axis, d))

    def scatter3(u, d):
        axis = orders[u][2]
        i = my(axis)
        return remote(t3.at[u, i], t3.at[u, i], s3s.at[u, d - 1], s3r.at[u, d - 1], along(axis, d))

    for u in range(UNITS):
        for d in (1, 2, 3):
            scatter1(c, u, d).wait_recv()
        mine = part[c, u, my(orders[u][0])] + r1[u, 0] + r1[u, 1] + r1[u, 2]
        for p in range(SIDE):
            s2[u, p] = mine[:, p * TILE : (p + 1) * TILE]
        for d in (2, 1, 3):
            scatter2(u, d).start()

    def exchange3():
        for u in range(UNITS):
            for d in (1, 2, 3):
                scatter2(u, d).wait_recv()
            t3[u, my(orders[u][2])] = s2[u, my(orders[u][1])] + r2[u, 0] + r2[u, 1] + r2[u, 2]
            for d in (2, 1, 3):
                scatter3(u, d).start()

    pl.when(c == 0)(exchange3)

    for copy in gram2_copies:
        copy.wait_recv()
    aug = gram2[0] + gram2[1] + gram2[2] + gram2[3]
    rows_at = lax.broadcasted_iota(jnp.int32, (R, 4 * R), 0)
    lanes_at = lax.broadcasted_iota(jnp.int32, (R, 4 * R), 1)
    unit_at = (lanes_at == rows_at + R) | (lanes_at == rows_at + 3 * R)
    aug = jnp.where(unit_at, 1.0, aug)
    first = lanes_at < 2 * R
    pivots = jnp.ones((R, 4 * R), jnp.float32)
    for k in range(R):
        column = jnp.where(first, aug[:, k : k + 1], aug[:, 2 * R + k : 2 * R + k + 1])
        pivot = column[k : k + 1, :]
        ratio = aug[k : k + 1, :] / pivot
        pivots = jnp.where(rows_at == k, pivot, pivots)
        aug = jnp.where(rows_at > k, aug - column * ratio, aug)
    aug = aug / jnp.sqrt(pivots)
    inverses = []
    for ex in range(EXP):
        wanted = (lanes_at >= (2 * ex + 1) * R) & (lanes_at < (2 * ex + 2) * R)
        inverses.append(jnp.where(wanted, aug, 0.0))
    aug_ref[0] = inverses[0]
    aug_ref[1] = inverses[1]

    pl.when(c == 1)(exchange3)

    for ex, panel in ((0, panel0), (1, panel1)):
        b = dot_high(inverses[ex], jnp.concatenate([panel] * 4, axis=0))
        hi, lo = [piece.astype(jnp.float32) for piece in split(b, 2)]
        basis[ex] = jnp.concatenate([hi, hi, lo, lo], axis=0).T.astype(jnp.bfloat16)

    def place(u):
        return c, u, my(orders[u][0]), my(orders[u][1])

    def gather2(u, d):
        spot = full.at[place(u)]
        return remote(spot, spot, a2s.at[u, d - 1], a2r.at[u, d - 1], along(orders[u][1], d))

    def gather1(u, d):
        spot = full.at[c, u, my(orders[u][0])]
        return remote(spot, spot, a1s.at[u, d - 1], a1r.at[u, d - 1], along(orders[u][0], d))

    def forward(ex, u, d):
        p = lax.rem(my(orders[u][0]) + d, SIDE)
        return remote(full.at[ex, u, p], full.at[ex, u, p], fs.at[u, d], fr.at[u, d], other)

    for u in range(UNITS):
        for d in (1, 2, 3):
            scatter3(u, d).wait_recv()
        tile = t3[u, 0] + t3[u, 1] + t3[u, 2] + t3[u, 3]
        full[place(u)] = dot_high(aug_ref[c], jnp.concatenate([tile] * 4, axis=0)) * (1.0 / REPS)
        for d in (2, 1, 3):
            gather2(u, d).start()
    for u in range(UNITS):
        for d in (1, 2, 3):
            gather2(u, d).wait_recv()
        for d in (2, 1, 3):
            gather1(u, d).start()
        forward(c, u, 0).start()

    def residual(ex, u):
        for p in range(SIDE):
            cols = pl.ds(u * UNIT + p * PIECE, PIECE)
            new = jnp.concatenate([full[ex, u, p, i] for i in range(SIDE)], axis=1)
            coeffs[ex, :, cols] = new
            hi, lo = split(new, 2)
            low = dot(basis[ex], jnp.concatenate([hi, lo, hi, lo], axis=0))
            merged = g[ex, :, cols].astype(jnp.float32) + e[ex, :, cols].astype(jnp.float32)
            fresh[0, ex, :, cols] = (merged - low).astype(jnp.bfloat16)

    def own_arrives(u):
        for d in (1, 3, 2):
            gather1(u, d).wait_recv()
            forward(c, u, SIDE - d).start()

    def other_arrives(u):
        for d in range(SIDE):
            forward(1 - c, u, d).wait_recv()

    for u in range(UNITS):
        own_arrives(u)
        residual(c, u)
    for u in range(UNITS):
        other_arrives(u)
        residual(1 - c, u)

    for ex in range(EXP):
        for d in (1, 2, 3):
            to_replica(ex, d).wait_send()
    for copy in gram1_copies + gram2_copies:
        copy.wait_send()
    for u in range(UNITS):
        to_partner(1 - c, u).wait_send()
        for d in range(SIDE):
            forward(c, u, d).wait_send()
        for d in (1, 2, 3):
            for copy in (scatter1(c, u, d), scatter2(u, d), scatter3(u, d), gather2(u, d), gather1(u, d)):
                copy.wait_send()


def store(fresh, coeffs, fresh_out, coeffs_out, sem):
    copies = [pltpu.make_async_copy(coeffs, coeffs_out, sem.at[EXP, 0])]
    for ex in range(EXP):
        for u in range(UNITS):
            spot = (0, ex, slice(None), pl.ds(u * UNIT, UNIT))
            copies.append(pltpu.make_async_copy(fresh.at[spot], fresh_out.at[spot], sem.at[ex, u]))
    for copy in copies:
        copy.start()
    for copy in copies:
        copy.wait()


def shards(grads, errors, q_init):
    dma = pltpu.SemaphoreType.DMA
    anywhere = pl.BlockSpec(memory_space=pl.ANY)
    vmem = pl.BlockSpec(memory_space=pltpu.VMEM)
    f32, b16 = jnp.float32, jnp.bfloat16
    fresh, coeffs = pl.pallas_call(
        kernel,
        out_shape=(
            pltpu.VMEM((1, EXP, ROWS, FF), b16),
            pltpu.VMEM((EXP, R, FF), f32),
        ),
        in_specs=[anywhere] * 3,
        out_specs=(vmem, vmem),
        scratch_shapes=[
            pltpu.VMEM((EXP, ROWS, FF), b16),
            pltpu.VMEM((EXP, ROWS, FF), b16),
            pltpu.VMEM((EXP, R, FF), f32),
            pltpu.VMEM((EXP, REPS, R + R // 2, LANES), f32),
            pltpu.VMEM((EXP, 3 * R, ROWS), b16),
            pltpu.VMEM((EXP, ROWS, 4 * R), b16),
            pltpu.VMEM((2 * SIDE, R, 4 * R), f32),
            pltpu.VMEM((SIDE, R, 4 * R), f32),
            pltpu.VMEM((EXP, R, 4 * R), f32),
            pltpu.VMEM((EXP, UNITS, SIDE, R, PIECE), f32),
            pltpu.VMEM((UNITS, SIDE, R, PIECE), f32),
            pltpu.VMEM((UNITS, SIDE - 1, R, PIECE), f32),
            pltpu.VMEM((UNITS, SIDE, R, TILE), f32),
            pltpu.VMEM((UNITS, SIDE - 1, R, TILE), f32),
            pltpu.VMEM((UNITS, SIDE, R, TILE), f32),
            pltpu.VMEM((EXP, UNITS, SIDE, SIDE, R, TILE), f32),
            dma((3, EXP, LOADS)),
            dma((EXP, 3)), dma((EXP, 3)),
            dma((7,)), dma((7,)), dma((3,)), dma((3,)),
            dma((UNITS,)), dma((UNITS,)),
            dma((UNITS, 3)), dma((UNITS, 3)),
            dma((UNITS, 3)), dma((UNITS, 3)),
            dma((UNITS, 3)), dma((UNITS, 3)),
            dma((UNITS, 3)), dma((UNITS, 3)),
            dma((UNITS, 3)), dma((UNITS, 3)),
            dma((UNITS, SIDE)), dma((UNITS, SIDE)),
        ],
        compiler_params=pltpu.CompilerParams(
            collective_id=0, has_side_effects=True, vmem_limit_bytes=48 * 2**20
        ),
        cost_estimate=pl.CostEstimate(flops=10**9, bytes_accessed=25 * 10**6, transcendentals=0),
        name="compress",
    )(grads, errors, q_init)
    return pl.pallas_call(
        store,
        out_shape=(
            jax.ShapeDtypeStruct((1, EXP, ROWS, FF), b16),
            jax.ShapeDtypeStruct((EXP, R, FF), f32),
        ),
        in_specs=[anywhere] * 2,
        out_specs=(anywhere, anywhere),
        scratch_shapes=[dma((EXP + 1, UNITS))],
        compiler_params=pltpu.CompilerParams(has_side_effects=True, vmem_limit_bytes=2**20),
        name="store",
    )(fresh, coeffs)


def solution(mesh):
    in_specs = (P("rep", None, "row", None), P("rep", None, "row", None), P())
    out_specs = (P("rep", None, "row", None), P())
    return jax.shard_map(shards, mesh=mesh, in_specs=in_specs, out_specs=out_specs, check_vma=False)
```

```python
import jax
import jax.numpy as jnp
from jax import lax
from jax.experimental import pallas as pl
from jax.experimental.pallas import tpu as pltpu
from jax.sharding import PartitionSpec as P

EXP, ROWS, FF, R = 2, 192, 8192, 32
REPS, SIDE = 4, 4
UNITS = 4
UNIT = FF // UNITS
PIECE = UNIT // SIDE
TILE = PIECE // SIDE
LANES = 128
LOADS = 2
LOAD = FF // LOADS
MESH = pl.DeviceIdType.MESH
HIGH = lax.Precision.HIGHEST
NN = (((1,), (0,)), ((), ()))
NT = (((1,), (1,)), ((), ()))


def split(value, pieces):
    out = []
    for _ in range(pieces):
        piece = value.astype(jnp.bfloat16)
        out.append(piece)
        value = value - piece.astype(jnp.float32)
    return out


def dot(a, b, dims=NN):
    return lax.dot_general(a, b, dims, preferred_element_type=jnp.float32)


def dot_high(a, b, dims=NN):
    return lax.dot_general(a, b, dims, precision=HIGH, preferred_element_type=jnp.float32)


def kernel(
    g_hbm, e_hbm, q_hbm, fresh, coeffs, g, e, basis,
    q, panels, left, gram1, gram2, aug_ref, part, partner, r1, s2, r2, t3, full,
    load_sem, ps, pr, g1s, g1r, g2s, g2r, cs, cr, s1s, s1r, s2s, s2r, s3s, s3r, a2s, a2r, a1s, a1r, fs, fr,
):
    y = lax.axis_index("rep")
    row = lax.axis_index("row")
    c = lax.rem(row, 2)
    z = lax.rem(row // 2, SIDE)
    x = row // (2 * SIDE)
    me = (x, y, z)

    def at(place, core):
        return (place[1], place[0] * (2 * SIDE) + place[2] * 2 + core)

    def along(axis, d):
        return at([lax.rem(p + d * w, SIDE) for p, w in zip(me, axis)], c)

    def my(axis):
        return x * axis[0] + y * axis[1] + z * axis[2]

    ax, ay, az = (1, 0, 0), (0, 1, 0), (0, 0, 1)

    def either(first, second):
        return [tuple(a * (1 - c) + b * c for a, b in zip(p, q)) for p, q in zip(first, second)]

    orders = [
        either((ax, ay, az), (az, ax, ay)),
        either((ay, az, ax), (ax, az, ay)),
        either((ay, az, ax), (ax, ay, az)),
        either((az, ax, ay), (ay, ax, az)),
    ]
    other = at(me, 1 - c)

    def remote(src, dst, send, recv, device):
        return pltpu.make_async_remote_copy(
            src_ref=src, dst_ref=dst, send_sem=send, recv_sem=recv, device_id=device, device_id_type=MESH
        )

    barrier = pltpu.get_barrier_semaphore()
    greeted = [along(axis, d) for axis in (ax, ay, az) for d in (1, 2, 3)]
    greeted += [at((lax.rem(x + d, SIDE), y, z), 1 - c) for d in range(SIDE)]
    for device in greeted:
        pl.semaphore_signal(barrier, inc=1, device_id=device, device_id_type=MESH)

    def loads(ex, h):
        cols = pl.ds(pl.multiple_of(h * LOAD, LOAD), LOAD)
        return [
            pltpu.make_async_copy(q_hbm.at[ex, :, cols], q.at[ex, :, cols], load_sem.at[0, ex, h]),
            pltpu.make_async_copy(g_hbm.at[0, ex, :, cols], g.at[ex, :, cols], load_sem.at[1, ex, h]),
            pltpu.make_async_copy(e_hbm.at[0, ex, :, cols], e.at[ex, :, cols], load_sem.at[2, ex, h]),
        ]

    for ex in range(EXP):
        for h in range(LOADS):
            for copy in loads(ex, h):
                copy.start()

    def to_replica(ex, d):
        spot = panels.at[ex, y]
        return remote(spot, spot, ps.at[ex, d - 1], pr.at[ex, d - 1], along(ay, d))

    def panel_term(ex, _):
        def add(h, total):
            for copy in loads(ex, h):
                copy.wait()
            cols = pl.ds(pl.multiple_of(h * LOAD, LOAD), LOAD)
            q3 = jnp.concatenate(split(q[ex, :, cols], 3), axis=0)
            return total + (dot(g[ex, :, cols], q3, NT) + dot(e[ex, :, cols], q3, NT))

        total = lax.fori_loop(0, LOADS, add, jnp.zeros((ROWS, 3 * R), jnp.float32))
        flat = jnp.concatenate([total, jnp.zeros((ROWS, R), jnp.float32)], axis=1).T
        term = flat[0:R] + flat[R : 2 * R] + flat[2 * R : 3 * R]
        panels[ex, y, 0:R] = term[:, 0:LANES]
        panels[ex, y, R:] = jnp.concatenate([term[: R // 2, LANES:], term[R // 2 :, LANES:]], axis=1)

        @pl.when(ex == 0)
        def _():
            pl.semaphore_wait(barrier, len(greeted))

        for d in (2, 1, 3):
            to_replica(ex, d).start()
        return 0

    lax.fori_loop(0, EXP, panel_term, 0)

    def finish_panel(ex):
        for d in (1, 2, 3):
            to_replica(ex, d).wait_recv()
        packed = (panels[ex, 0] + panels[ex, 1] + panels[ex, 2] + panels[ex, 3]) * (1.0 / REPS)
        rest = packed[R:]
        rest = jnp.concatenate([rest[:, : LANES // 2], rest[:, LANES // 2 :]], axis=0)
        panel = jnp.concatenate([packed[0:R], rest], axis=1)
        left[ex] = jnp.concatenate(split(panel, 3), axis=0)
        return panel

    def unit(j):
        return j // 2, 2 * c + j % 2

    def unit_there(j):
        return j // 2, 2 * (1 - c) + j % 2

    def product(ex, u, p):
        cols = pl.ds(pl.multiple_of(u * UNIT + p * PIECE, PIECE), PIECE)
        both = dot(left[ex], g[ex, :, cols]) + dot(left[ex], e[ex, :, cols])
        part[ex, u, p] = both[0:R] + both[R : 2 * R] + both[2 * R : 3 * R]

    def to_partner(j, p):
        spot = part.at[(*unit_there(j), p)]
        return remote(spot, partner.at[j, p], cs.at[j, p], cr.at[j, p], other)

    def scatter1(j, d):
        axis = orders[j][0]
        p = lax.rem(my(axis) + d, SIDE)
        spot = part.at[(*unit(j), p)]
        return remote(spot, r1.at[j, d - 1], s1s.at[j, d - 1], s1r.at[j, d - 1], along(axis, d))

    def coefficients(ex):
        for j in (2 * ex, 2 * ex + 1):
            for p in range(SIDE):
                product(*unit_there(j), p)
            for p in range(SIDE):
                to_partner(j, p).start()
        for j in (2 * ex, 2 * ex + 1):
            for p in range(SIDE):
                product(*unit(j), p)
            for p in range(SIDE):
                to_partner(j, p).wait_recv()
                spot = (*unit(j), p)
                part[spot] = part[spot] + partner[j, p]
            for d in (2, 1, 3):
                scatter1(j, d).start()

    panel0 = finish_panel(0)
    coefficients(0)
    panel1 = finish_panel(1)

    zeros = jnp.zeros((R, ROWS), jnp.float32)
    pad0 = jnp.concatenate([panel0, zeros, zeros, zeros], axis=0)
    pad1 = jnp.concatenate([zeros, zeros, panel1, zeros], axis=0)
    gram1[2 * x + c] = dot_high(panel0, pad0, NT) + dot_high(panel1, pad1, NT)
    gram1_copies = []
    for i in range(7):
        if i < 3:
            device = along(ax, i + 1)
        else:
            device = at((lax.rem(x + i - 3, SIDE), y, z), 1 - c)
        copy = remote(gram1.at[2 * x + c], gram1.at[2 * x + c], g1s.at[i], g1r.at[i], device)
        copy.start()
        gram1_copies.append(copy)

    coefficients(1)

    def scatter2(j, d):
        axis = orders[j][1]
        p = lax.rem(my(axis) + d, SIDE)
        return remote(s2.at[j, p], r2.at[j, d - 1], s2s.at[j, d - 1], s2r.at[j, d - 1], along(axis, d))

    def scatter3(j, d):
        axis = orders[j][2]
        i = my(axis)
        return remote(t3.at[j, i], t3.at[j, i], s3s.at[j, d - 1], s3r.at[j, d - 1], along(axis, d))

    def gather2(j, d):
        spot = full.at[(*unit(j), my(orders[j][0]), my(orders[j][1]))]
        return remote(spot, spot, a2s.at[j, d - 1], a2r.at[j, d - 1], along(orders[j][1], d))

    def gather1(j, d):
        spot = full.at[(*unit(j), my(orders[j][0]))]
        return remote(spot, spot, a1s.at[j, d - 1], a1r.at[j, d - 1], along(orders[j][0], d))

    def forward(j, d):
        spot = full.at[(*unit(j), lax.rem(my(orders[j][0]) + d, SIDE))]
        return remote(spot, spot, fs.at[j, d], fr.at[j, d], other)

    def exchange2(ex):
        for j in (2 * ex, 2 * ex + 1):
            for d in (1, 3, 2):
                scatter1(j, d).wait_recv()
            mine = part[(*unit(j), my(orders[j][0]))] + r1[j, 0] + r1[j, 1] + r1[j, 2]
            for p in range(SIDE):
                s2[j, p] = mine[:, p * TILE : (p + 1) * TILE]
            for d in (2, 1, 3):
                scatter2(j, d).start()

    def exchange3(ex):
        for j in (2 * ex, 2 * ex + 1):
            for d in (1, 3, 2):
                scatter2(j, d).wait_recv()
            t3[j, my(orders[j][2])] = s2[j, my(orders[j][1])] + r2[j, 0] + r2[j, 1] + r2[j, 2]
            for d in (2, 1, 3):
                scatter3(j, d).start()

    def own_tile(ex):
        for j in (2 * ex, 2 * ex + 1):
            for d in (1, 3, 2):
                scatter3(j, d).wait_recv()
            tile = t3[j, 0] + t3[j, 1] + t3[j, 2] + t3[j, 3]
            new = dot_high(aug_ref[ex], jnp.concatenate([tile] * 4, axis=0)) * (1.0 / REPS)
            full[(*unit(j), my(orders[j][0]), my(orders[j][1]))] = new
            for d in (2, 1, 3):
                gather2(j, d).start()

    def spread(ex):
        for j in (2 * ex, 2 * ex + 1):
            for d in (1, 3, 2):
                gather2(j, d).wait_recv()
            for d in (2, 1, 3):
                gather1(j, d).start()
            forward(j, 0).start()

    for copy in gram1_copies:
        copy.wait_recv()
    total = gram1[0]
    for i in range(1, 2 * SIDE):
        total += gram1[i]
    gram2[z] = total
    gram2_copies = []
    for d in (2, 1, 3):
        copy = remote(gram2.at[z], gram2.at[z], g2s.at[d - 1], g2r.at[d - 1], along(az, d))
        copy.start()
        gram2_copies.append(copy)

    exchange2(0)
    exchange2(1)
    exchange3(0)

    for copy in gram2_copies:
        copy.wait_recv()
    aug = gram2[0] + gram2[1] + gram2[2] + gram2[3]
    rows_at = lax.broadcasted_iota(jnp.int32, (R, 4 * R), 0)
    lanes_at = lax.broadcasted_iota(jnp.int32, (R, 4 * R), 1)
    unit_at = (lanes_at == rows_at + R) | (lanes_at == rows_at + 3 * R)
    aug = jnp.where(unit_at, 1.0, aug)
    first = lanes_at < 2 * R
    pivots = jnp.ones((R, 4 * R), jnp.float32)
    for k in range(0, R, 2):
        col = [jnp.where(first, aug[:, i : i + 1], aug[:, 2 * R + i : 2 * R + i + 1]) for i in (k, k + 1)]
        row = [aug[i : i + 1, :] for i in (k, k + 1)]
        top, side, low = col[0][k : k + 1, :], col[0][k + 1 : k + 2, :], col[1][k + 1 : k + 2, :]
        scale = side / top
        ratio = row[0] / top
        below = row[1] - scale * row[0]
        pivot = low - scale * side
        col[1] = col[1] - col[0] * scale
        pivots = jnp.where(rows_at == k, top, jnp.where(rows_at == k + 1, pivot, pivots))
        rest = aug - col[0] * ratio - col[1] * (below / pivot)
        aug = jnp.where(rows_at > k + 1, rest, jnp.where(rows_at == k + 1, below, aug))
    aug = aug / jnp.sqrt(pivots)
    for ex in range(EXP):
        wanted = (lanes_at >= (2 * ex + 1) * R) & (lanes_at < (2 * ex + 2) * R)
        aug_ref[ex] = jnp.where(wanted, aug, 0.0)

    exchange3(1)
    own_tile(0)

    for ex, panel in ((0, panel0), (1, panel1)):
        b = dot_high(aug_ref[ex], jnp.concatenate([panel] * 4, axis=0))
        hi, lo = [piece.astype(jnp.float32) for piece in split(b, 2)]
        basis[ex] = jnp.concatenate([hi, hi, lo, lo], axis=0).T.astype(jnp.bfloat16)

    own_tile(1)
    spread(0)
    spread(1)

    def finish_unit(ex, u):
        for p in range(SIDE):
            cols = pl.ds(pl.multiple_of(u * UNIT + p * PIECE, PIECE), PIECE)
            coeffs[ex, :, cols] = jnp.concatenate([full[ex, u, p, i] for i in range(SIDE)], axis=1)
            if ex == 0:
                fresh[:, cols] = residual(g, e, basis, coeffs, ex, cols)

    for ex in range(EXP):
        for j in (2 * ex, 2 * ex + 1):
            for d in (1, 3, 2):
                gather1(j, d).wait_recv()
                forward(j, SIDE - d).start()
            finish_unit(*unit(j))
        for j in (2 * ex, 2 * ex + 1):
            for d in range(SIDE):
                forward(j, d).wait_recv()
            finish_unit(*unit_there(j))

    for ex in range(EXP):
        for d in (1, 2, 3):
            to_replica(ex, d).wait_send()
    for copy in gram1_copies + gram2_copies:
        copy.wait_send()
    for j in range(UNITS):
        for d in range(SIDE):
            to_partner(j, d).wait_send()
            forward(j, d).wait_send()
        for d in (1, 2, 3):
            for copy in (scatter1(j, d), scatter2(j, d), scatter3(j, d), gather2(j, d), gather1(j, d)):
                copy.wait_send()


def residual(g, e, basis, coeffs, ex, cols):
    hi, lo = split(coeffs[ex, :, cols], 2)
    low = dot(basis[ex], jnp.concatenate([hi, lo, hi, lo], axis=0))
    merged = g[ex, :, cols].astype(jnp.float32) + e[ex, :, cols].astype(jnp.float32)
    return (merged - low).astype(jnp.bfloat16)


def store(fresh0, coeffs, g, e, basis, fresh_out, coeffs_out, fresh1, sem):
    copies = []

    def send(src, dst):
        copies.append(pltpu.make_async_copy(src, dst, sem.at[len(copies)]))
        copies[-1].start()

    units = [pl.ds(u * UNIT, UNIT) for u in range(UNITS)]
    for cols in units:
        send(fresh0.at[:, cols], fresh_out.at[0, 0, :, cols])
    for ex in range(EXP):
        send(coeffs.at[ex], coeffs_out.at[ex])
    for u in range(UNITS):
        for p in range(SIDE):
            cols = pl.ds(u * UNIT + p * PIECE, PIECE)
            fresh1[:, cols] = residual(g, e, basis, coeffs, 1, cols)
        send(fresh1.at[:, units[u]], fresh_out.at[0, 1, :, units[u]])
    for copy in copies:
        copy.wait()


def shards(grads, errors, q_init):
    dma = pltpu.SemaphoreType.DMA
    anywhere = pl.BlockSpec(memory_space=pl.ANY)
    vmem = pl.BlockSpec(memory_space=pltpu.VMEM)
    f32, b16 = jnp.float32, jnp.bfloat16
    held = pl.pallas_call(
        kernel,
        out_shape=(
            pltpu.VMEM((ROWS, FF), b16),
            pltpu.VMEM((EXP, R, FF), f32),
            pltpu.VMEM((EXP, ROWS, FF), b16),
            pltpu.VMEM((EXP, ROWS, FF), b16),
            pltpu.VMEM((EXP, ROWS, 4 * R), b16),
        ),
        in_specs=[anywhere] * 3,
        out_specs=(vmem,) * 5,
        scratch_shapes=[
            pltpu.VMEM((EXP, R, FF), f32),
            pltpu.VMEM((EXP, REPS, R + R // 2, LANES), f32),
            pltpu.VMEM((EXP, 3 * R, ROWS), b16),
            pltpu.VMEM((2 * SIDE, R, 4 * R), f32),
            pltpu.VMEM((SIDE, R, 4 * R), f32),
            pltpu.VMEM((EXP, R, 4 * R), f32),
            pltpu.VMEM((EXP, UNITS, SIDE, R, PIECE), f32),
            pltpu.VMEM((UNITS, SIDE, R, PIECE), f32),
            pltpu.VMEM((UNITS, SIDE - 1, R, PIECE), f32),
            pltpu.VMEM((UNITS, SIDE, R, TILE), f32),
            pltpu.VMEM((UNITS, SIDE - 1, R, TILE), f32),
            pltpu.VMEM((UNITS, SIDE, R, TILE), f32),
            pltpu.VMEM((EXP, UNITS, SIDE, SIDE, R, TILE), f32),
            dma((3, EXP, LOADS)),
            dma((EXP, 3)), dma((EXP, 3)),
            dma((7,)), dma((7,)), dma((3,)), dma((3,)),
            dma((UNITS, SIDE)), dma((UNITS, SIDE)),
            dma((UNITS, 3)), dma((UNITS, 3)),
            dma((UNITS, 3)), dma((UNITS, 3)),
            dma((UNITS, 3)), dma((UNITS, 3)),
            dma((UNITS, 3)), dma((UNITS, 3)),
            dma((UNITS, 3)), dma((UNITS, 3)),
            dma((UNITS, SIDE)), dma((UNITS, SIDE)),
        ],
        compiler_params=pltpu.CompilerParams(
            collective_id=0, has_side_effects=True, vmem_limit_bytes=44 * 2**20
        ),
        cost_estimate=pl.CostEstimate(flops=10**9, bytes_accessed=25 * 10**6, transcendentals=0),
        name="compress",
    )(grads, errors, q_init)
    return pl.pallas_call(
        store,
        out_shape=(
            jax.ShapeDtypeStruct((1, EXP, ROWS, FF), b16),
            jax.ShapeDtypeStruct((EXP, R, FF), f32),
        ),
        in_specs=[anywhere] + [vmem] * 4,
        out_specs=(anywhere, anywhere),
        scratch_shapes=[pltpu.VMEM((ROWS, FF), b16), dma((2 * UNITS + EXP,))],
        compiler_params=pltpu.CompilerParams(has_side_effects=True, vmem_limit_bytes=8 * 2**20),
        name="store",
    )(*held)


def solution(mesh):
    in_specs = (P("rep", None, "row", None), P("rep", None, "row", None), P())
    out_specs = (P("rep", None, "row", None), P())
    return jax.shard_map(shards, mesh=mesh, in_specs=in_specs, out_specs=out_specs, check_vma=False)
```

```python
import jax
import jax.numpy as jnp
from jax import lax
from jax.experimental import pallas as pl
from jax.experimental.pallas import tpu as pltpu
from jax.sharding import PartitionSpec as P

EXP, ROWS, FF, R = 2, 192, 8192, 32
REPS, SIDE = 4, 4
UNITS = 4
STREAMS = 6
UNIT = FF // UNITS
PIECE = UNIT // SIDE
TILE = PIECE // SIDE
LANES = 128
LOADS = 4
LOAD = FF // LOADS
MESH = pl.DeviceIdType.MESH
HIGH = lax.Precision.HIGHEST
NN = (((1,), (0,)), ((), ()))
NT = (((1,), (1,)), ((), ()))


def split(value, pieces):
    out = []
    for _ in range(pieces):
        piece = value.astype(jnp.bfloat16)
        out.append(piece)
        value = value - piece.astype(jnp.float32)
    return out


def dot(a, b, dims=NN):
    return lax.dot_general(a, b, dims, preferred_element_type=jnp.float32)


def dot_high(a, b, dims=NN):
    return lax.dot_general(a, b, dims, precision=HIGH, preferred_element_type=jnp.float32)


def kernel(
    g_hbm, e_hbm, q_hbm, fresh, coeffs, g, e, basis,
    q, panels, left, gram1, gram2, aug_ref, part, partner, r1, r1b, s2, r2, t3, full,
    load_sem, ps, pr, g1s, g1r, g2s, g2r, cs, cr, s1s, s1r, s2s, s2r, s3s, s3r, a2s, a2r, a1s, a1r, fs, fr,
):
    y = lax.axis_index("rep")
    row = lax.axis_index("row")
    c = lax.rem(row, 2)
    z = lax.rem(row // 2, SIDE)
    x = row // (2 * SIDE)
    me = (x, y, z)

    def at(place, core):
        return (place[1], place[0] * (2 * SIDE) + place[2] * 2 + core)

    def along(axis, d):
        return at([lax.rem(p + d * w, SIDE) for p, w in zip(me, axis)], c)

    def my(axis):
        return x * axis[0] + y * axis[1] + z * axis[2]

    ax, ay, az = (1, 0, 0), (0, 1, 0), (0, 0, 1)

    def either(first, second, core=c):
        return [tuple(a * (1 - core) + b * core for a, b in zip(p, q)) for p, q in zip(first, second)]

    table = [
        ((ax, ay, az), (ay, az, ax)),
        ((az, ax, ay), (az, ay, ax)),
        ((ay, az, ax), (az, ax, ay)),
        ((ax, ay, az), (ax, az, ay)),
    ]
    orders = [either(*pair) for pair in table]
    orders_there = [either(*pair, 1 - c) for pair in table]
    streams = []
    for j in range(UNITS):
        if j % 2 == 0:
            streams.append((j, pl.ds(0, R), 0, 1))
        else:
            streams.append((j, pl.ds(0, R // 2), 0, 1))
            streams.append((j, pl.ds(R // 2, R // 2), 1, 0))

    def streams_of(ex):
        return [s for s, stream in enumerate(streams) if stream[0] // 2 == ex]

    def axes(s):
        j, _, a, b = streams[s]
        return orders[j][a], orders[j][b]

    def shifted(axis, d):
        return lax.rem(my(axis) + d, SIDE)

    other = at(me, 1 - c)

    def remote(src, dst, send, recv, device):
        return pltpu.make_async_remote_copy(
            src_ref=src, dst_ref=dst, send_sem=send, recv_sem=recv, device_id=device, device_id_type=MESH
        )

    barrier = pltpu.get_barrier_semaphore()
    greeted = [along(axis, d) for axis in (ax, ay, az) for d in (1, 2, 3)]
    greeted += [at((lax.rem(x + d, SIDE), y, z), 1 - c) for d in range(SIDE)]
    for device in greeted:
        pl.semaphore_signal(barrier, inc=1, device_id=device, device_id_type=MESH)

    def loads(ex, h):
        cols = pl.ds(pl.multiple_of(h * LOAD, LOAD), LOAD)
        return [
            pltpu.make_async_copy(q_hbm.at[ex, :, cols], q.at[ex, :, cols], load_sem.at[0, ex, h]),
            pltpu.make_async_copy(g_hbm.at[0, ex, :, cols], g.at[ex, :, cols], load_sem.at[1, ex, h]),
            pltpu.make_async_copy(e_hbm.at[0, ex, :, cols], e.at[ex, :, cols], load_sem.at[2, ex, h]),
        ]

    for ex in range(EXP):
        for h in range(LOADS):
            for copy in loads(ex, h):
                copy.start()

    def to_replica(ex, d):
        spot = panels.at[ex, y]
        return remote(spot, spot, ps.at[ex, d - 1], pr.at[ex, d - 1], along(ay, d))

    def panel_term(ex, _):
        def add(h, total):
            for copy in loads(ex, h):
                copy.wait()
            cols = pl.ds(pl.multiple_of(h * LOAD, LOAD), LOAD)
            q3 = jnp.concatenate(split(q[ex, :, cols], 3), axis=0)
            return total + (dot(g[ex, :, cols], q3, NT) + dot(e[ex, :, cols], q3, NT))

        total = lax.fori_loop(0, LOADS, add, jnp.zeros((ROWS, 3 * R), jnp.float32))
        flat = jnp.concatenate([total, jnp.zeros((ROWS, R), jnp.float32)], axis=1).T
        term = flat[0:R] + flat[R : 2 * R] + flat[2 * R : 3 * R]
        panels[ex, y, 0:R] = term[:, 0:LANES]
        panels[ex, y, R:] = jnp.concatenate([term[: R // 2, LANES:], term[R // 2 :, LANES:]], axis=1)

        @pl.when(ex == 0)
        def _():
            pl.semaphore_wait(barrier, len(greeted))

        for d in (2, 1, 3):
            to_replica(ex, d).start()
        return 0

    lax.fori_loop(0, EXP, panel_term, 0)

    def finish_panel(ex):
        for d in (1, 2, 3):
            to_replica(ex, d).wait_recv()
        packed = (panels[ex, 0] + panels[ex, 1] + panels[ex, 2] + panels[ex, 3]) * (1.0 / REPS)
        rest = packed[R:]
        rest = jnp.concatenate([rest[:, : LANES // 2], rest[:, LANES // 2 :]], axis=0)
        panel = jnp.concatenate([packed[0:R], rest], axis=1)
        left[ex] = jnp.concatenate(split(panel, 3), axis=0)
        return panel

    def unit(j):
        return j // 2, 2 * c + j % 2

    def unit_there(j):
        return j // 2, 2 * (1 - c) + j % 2

    def product(ex, u, p):
        cols = pl.ds(pl.multiple_of(u * UNIT + p * PIECE, PIECE), PIECE)
        both = dot(left[ex], g[ex, :, cols]) + dot(left[ex], e[ex, :, cols])
        part[ex, u, p] = both[0:R] + both[R : 2 * R] + both[2 * R : 3 * R]

    def to_partner(j, p):
        spot = part.at[(*unit_there(j), p)]
        return remote(spot, partner.at[j, p], cs.at[j, p], cr.at[j, p], other)

    def lanes(p):
        return pl.ds(pl.multiple_of(p * TILE, TILE), TILE)

    def scatter1(s, d):
        j, rows, swapped, _ = streams[s]
        axis = axes(s)[0]
        p = shifted(axis, d)
        if swapped:
            src, dst = part.at[(*unit(j), slice(None), rows, lanes(p))], r1b.at[j // 2, d - 1]
        else:
            src, dst = part.at[(*unit(j), p, rows)], r1.at[j, d - 1, rows]
        return remote(src, dst, s1s.at[s, d - 1], s1r.at[s, d - 1], along(axis, d))

    def coefficients(ex):
        units = (2 * ex, 2 * ex + 1)
        for j in units:
            for p in range(SIDE):
                product(*unit_there(j), p)
            for d in (2, 1, 3, 0):
                to_partner(j, shifted(orders_there[j][0], d)).start()
        for j in units:
            for p in range(SIDE):
                product(*unit(j), p)
        for j in units:
            mine = [s for s in streams_of(ex) if streams[s][0] == j]
            for d in (2, 1, 3, 0):
                p = shifted(orders[j][0], d)
                to_partner(j, p).wait_recv()
                spot = (*unit(j), p)
                part[spot] = part[spot] + partner[j, p]
                if d:
                    scatter1(mine[0], d).start()
            for s in mine[1:]:
                for d in (2, 1, 3):
                    scatter1(s, d).start()

    panel0 = finish_panel(0)
    coefficients(0)
    panel1 = finish_panel(1)

    zeros = jnp.zeros((R, ROWS), jnp.float32)
    pad0 = jnp.concatenate([panel0, zeros, zeros, zeros], axis=0)
    pad1 = jnp.concatenate([zeros, zeros, panel1, zeros], axis=0)
    gram1[2 * x + c] = dot_high(panel0, pad0, NT) + dot_high(panel1, pad1, NT)
    gram1_copies = []
    for i in range(7):
        if i < 3:
            device = along(ax, i + 1)
        else:
            device = at((lax.rem(x + i - 3, SIDE), y, z), 1 - c)
        copy = remote(gram1.at[2 * x + c], gram1.at[2 * x + c], g1s.at[i], g1r.at[i], device)
        copy.start()
        gram1_copies.append(copy)

    coefficients(1)

    def scatter2(s, d):
        j, rows, _, _ = streams[s]
        axis = axes(s)[1]
        src, dst = s2.at[j, shifted(axis, d), rows], r2.at[j, d - 1, rows]
        return remote(src, dst, s2s.at[s, d - 1], s2r.at[s, d - 1], along(axis, d))

    def scatter3(j, d):
        axis = orders[j][2]
        i = my(axis)
        return remote(t3.at[j, i], t3.at[j, i], s3s.at[j, d - 1], s3r.at[j, d - 1], along(axis, d))

    def gather2(s, d):
        j, rows, _, _ = streams[s]
        axis = axes(s)[1]
        spot = full.at[(*unit(j), my(orders[j][0]), my(orders[j][1]), rows)]
        return remote(spot, spot, a2s.at[s, d - 1], a2r.at[s, d - 1], along(axis, d))

    def band(s, p):
        j, rows, swapped, _ = streams[s]
        if swapped:
            return full.at[(*unit(j), slice(None), p, rows)]
        return full.at[(*unit(j), p, slice(None), rows)]

    def gather1(s, d):
        axis = axes(s)[0]
        spot = band(s, my(axis))
        return remote(spot, spot, a1s.at[s, d - 1], a1r.at[s, d - 1], along(axis, d))

    def forward(s, d):
        spot = band(s, shifted(axes(s)[0], d))
        return remote(spot, spot, fs.at[s, d], fr.at[s, d], other)

    def exchange2(ex):
        for s in streams_of(ex):
            j, rows, swapped, _ = streams[s]
            for d in (1, 3, 2):
                scatter1(s, d).wait_recv()
            p = my(axes(s)[0])
            if swapped:
                for i in range(SIDE):
                    mine = part[(*unit(j), i, rows, lanes(p))]
                    s2[j, i, rows] = mine + r1b[ex, 0, i] + r1b[ex, 1, i] + r1b[ex, 2, i]
            else:
                mine = part[(*unit(j), p, rows)] + r1[j, 0, rows] + r1[j, 1, rows] + r1[j, 2, rows]
                for i in range(SIDE):
                    s2[j, i, rows] = mine[:, i * TILE : (i + 1) * TILE]
            for d in (2, 1, 3):
                scatter2(s, d).start()

    def exchange3(ex):
        for j in (2 * ex, 2 * ex + 1):
            for s in streams_of(ex):
                if streams[s][0] == j:
                    rows = streams[s][1]
                    for d in (1, 3, 2):
                        scatter2(s, d).wait_recv()
                    mine = s2[j, my(axes(s)[1]), rows]
                    t3[j, my(orders[j][2]), rows] = mine + r2[j, 0, rows] + r2[j, 1, rows] + r2[j, 2, rows]
            for d in (2, 1, 3):
                scatter3(j, d).start()

    def own_tile(ex):
        for j in (2 * ex, 2 * ex + 1):
            for d in (1, 3, 2):
                scatter3(j, d).wait_recv()
            tile = t3[j, 0] + t3[j, 1] + t3[j, 2] + t3[j, 3]
            new = dot_high(aug_ref[ex], jnp.concatenate([tile] * 4, axis=0)) * (1.0 / REPS)
            full[(*unit(j), my(orders[j][0]), my(orders[j][1]))] = new
            for s in streams_of(ex):
                if streams[s][0] == j:
                    for d in (2, 1, 3):
                        gather2(s, d).start()

    def spread(ex):
        for s in streams_of(ex):
            for d in (1, 3, 2):
                gather2(s, d).wait_recv()
            for d in (2, 1, 3):
                gather1(s, d).start()
            forward(s, 0).start()

    exchange2(0)
    for copy in gram1_copies:
        copy.wait_recv()
    total = gram1[0]
    for i in range(1, 2 * SIDE):
        total += gram1[i]
    gram2[z] = total
    gram2_copies = []
    for d in (2, 1, 3):
        copy = remote(gram2.at[z], gram2.at[z], g2s.at[d - 1], g2r.at[d - 1], along(az, d))
        copy.start()
        gram2_copies.append(copy)

    exchange2(1)
    exchange3(0)

    exchange3(1)

    for copy in gram2_copies:
        copy.wait_recv()
    aug = gram2[0] + gram2[1] + gram2[2] + gram2[3]
    rows_at = lax.broadcasted_iota(jnp.int32, (R, 4 * R), 0)
    lanes_at = lax.broadcasted_iota(jnp.int32, (R, 4 * R), 1)
    unit_at = (lanes_at == rows_at + R) | (lanes_at == rows_at + 3 * R)
    aug = jnp.where(unit_at, 1.0, aug)
    first = lanes_at < 2 * R
    pivots = jnp.ones((R, 4 * R), jnp.float32)
    for k in range(0, R, 2):
        col = [jnp.where(first, aug[:, i : i + 1], aug[:, 2 * R + i : 2 * R + i + 1]) for i in (k, k + 1)]
        row = [aug[i : i + 1, :] for i in (k, k + 1)]
        top, side, low = col[0][k : k + 1, :], col[0][k + 1 : k + 2, :], col[1][k + 1 : k + 2, :]
        scale = side / top
        ratio = row[0] / top
        below = row[1] - scale * row[0]
        pivot = low - scale * side
        col[1] = col[1] - col[0] * scale
        pivots = jnp.where(rows_at == k, top, jnp.where(rows_at == k + 1, pivot, pivots))
        rest = aug - col[0] * ratio - col[1] * (below / pivot)
        aug = jnp.where(rows_at > k + 1, rest, jnp.where(rows_at == k + 1, below, aug))
    aug = aug / jnp.sqrt(pivots)
    for ex in range(EXP):
        wanted = (lanes_at >= (2 * ex + 1) * R) & (lanes_at < (2 * ex + 2) * R)
        aug_ref[ex] = jnp.where(wanted, aug, 0.0)

    own_tile(0)

    own_tile(1)
    for ex, panel in ((0, panel0), (1, panel1)):
        b = dot_high(aug_ref[ex], jnp.concatenate([panel] * 4, axis=0))
        hi, lo = [piece.astype(jnp.float32) for piece in split(b, 2)]
        basis[ex] = jnp.concatenate([hi, hi, lo, lo], axis=0).T.astype(jnp.bfloat16)

    spread(0)
    spread(1)

    def finish_unit(ex, u, errors):
        for p in range(SIDE):
            cols = pl.ds(pl.multiple_of(u * UNIT + p * PIECE, PIECE), PIECE)
            coeffs[ex, :, cols] = jnp.concatenate([full[ex, u, p, i] for i in range(SIDE)], axis=1)
            if errors:
                fresh[:, cols] = residual(g, e, basis, coeffs, ex, cols)

    for ex in range(EXP):
        for j in (2 * ex, 2 * ex + 1):
            for s in streams_of(ex):
                if streams[s][0] == j:
                    for d in (1, 3, 2):
                        gather1(s, d).wait_recv()
                        forward(s, SIDE - d).start()
            finish_unit(*unit(j), ex == 0)
    for j in range(UNITS):
        for s in streams_of(j // 2):
            if streams[s][0] == j:
                for d in range(SIDE):
                    forward(s, d).wait_recv()
        finish_unit(*unit_there(j), j < 2)

    for ex in range(EXP):
        for d in (1, 2, 3):
            to_replica(ex, d).wait_send()
    for copy in gram1_copies + gram2_copies:
        copy.wait_send()
    for j in range(UNITS):
        for d in range(SIDE):
            to_partner(j, d).wait_send()
        for d in (1, 2, 3):
            scatter3(j, d).wait_send()
    for s in range(len(streams)):
        for d in range(SIDE):
            forward(s, d).wait_send()
        for d in (1, 2, 3):
            for copy in (scatter1(s, d), scatter2(s, d), gather2(s, d), gather1(s, d)):
                copy.wait_send()


def residual(g, e, basis, coeffs, ex, cols):
    hi, lo = split(coeffs[ex, :, cols], 2)
    low = dot(basis[ex], jnp.concatenate([hi, lo, hi, lo], axis=0))
    merged = g[ex, :, cols].astype(jnp.float32) + e[ex, :, cols].astype(jnp.float32)
    return (merged - low).astype(jnp.bfloat16)


def store(fresh0, coeffs, g, e, basis, fresh_out, coeffs_out, fresh1, sem):
    copies = []

    def send(src, dst):
        copies.append(pltpu.make_async_copy(src, dst, sem.at[len(copies)]))
        copies[-1].start()

    units = [pl.ds(u * UNIT, UNIT) for u in range(UNITS)]
    for cols in units:
        send(fresh0.at[:, cols], fresh_out.at[0, 0, :, cols])
    for ex in range(EXP):
        send(coeffs.at[ex], coeffs_out.at[ex])
    for u in range(UNITS):
        for p in range(SIDE):
            cols = pl.ds(u * UNIT + p * PIECE, PIECE)
            fresh1[:, cols] = residual(g, e, basis, coeffs, 1, cols)
        send(fresh1.at[:, units[u]], fresh_out.at[0, 1, :, units[u]])
    for copy in copies:
        copy.wait()


def shards(grads, errors, q_init):
    dma = pltpu.SemaphoreType.DMA
    anywhere = pl.BlockSpec(memory_space=pl.ANY)
    vmem = pl.BlockSpec(memory_space=pltpu.VMEM)
    f32, b16 = jnp.float32, jnp.bfloat16
    held = pl.pallas_call(
        kernel,
        out_shape=(
            pltpu.VMEM((ROWS, FF), b16),
            pltpu.VMEM((EXP, R, FF), f32),
            pltpu.VMEM((EXP, ROWS, FF), b16),
            pltpu.VMEM((EXP, ROWS, FF), b16),
            pltpu.VMEM((EXP, ROWS, 4 * R), b16),
        ),
        in_specs=[anywhere] * 3,
        out_specs=(vmem,) * 5,
        scratch_shapes=[
            pltpu.VMEM((EXP, R, FF), f32),
            pltpu.VMEM((EXP, REPS, R + R // 2, LANES), f32),
            pltpu.VMEM((EXP, 3 * R, ROWS), b16),
            pltpu.VMEM((2 * SIDE, R, 4 * R), f32),
            pltpu.VMEM((SIDE, R, 4 * R), f32),
            pltpu.VMEM((EXP, R, 4 * R), f32),
            pltpu.VMEM((EXP, UNITS, SIDE, R, PIECE), f32),
            pltpu.VMEM((UNITS, SIDE, R, PIECE), f32),
            pltpu.VMEM((UNITS, SIDE - 1, R, PIECE), f32),
            pltpu.VMEM((EXP, SIDE - 1, SIDE, R // 2, TILE), f32),
            pltpu.VMEM((UNITS, SIDE, R, TILE), f32),
            pltpu.VMEM((UNITS, SIDE - 1, R, TILE), f32),
            pltpu.VMEM((UNITS, SIDE, R, TILE), f32),
            pltpu.VMEM((EXP, UNITS, SIDE, SIDE, R, TILE), f32),
            dma((3, EXP, LOADS)),
            dma((EXP, 3)), dma((EXP, 3)),
            dma((7,)), dma((7,)), dma((3,)), dma((3,)),
            dma((UNITS, SIDE)), dma((UNITS, SIDE)),
            dma((STREAMS, 3)), dma((STREAMS, 3)),
            dma((STREAMS, 3)), dma((STREAMS, 3)),
            dma((UNITS, 3)), dma((UNITS, 3)),
            dma((STREAMS, 3)), dma((STREAMS, 3)),
            dma((STREAMS, 3)), dma((STREAMS, 3)),
            dma((STREAMS, SIDE)), dma((STREAMS, SIDE)),
        ],
        compiler_params=pltpu.CompilerParams(
            collective_id=0, has_side_effects=True, vmem_limit_bytes=44 * 2**20
        ),
        cost_estimate=pl.CostEstimate(flops=10**9, bytes_accessed=25 * 10**6, transcendentals=0),
        name="compress",
    )(grads, errors, q_init)
    return pl.pallas_call(
        store,
        out_shape=(
            jax.ShapeDtypeStruct((1, EXP, ROWS, FF), b16),
            jax.ShapeDtypeStruct((EXP, R, FF), f32),
        ),
        in_specs=[anywhere] + [vmem] * 4,
        out_specs=(anywhere, anywhere),
        scratch_shapes=[pltpu.VMEM((ROWS, FF), b16), dma((2 * UNITS + EXP,))],
        compiler_params=pltpu.CompilerParams(has_side_effects=True, vmem_limit_bytes=8 * 2**20),
        name="store",
    )(*held)


def solution(mesh):
    in_specs = (P("rep", None, "row", None), P("rep", None, "row", None), P())
    out_specs = (P("rep", None, "row", None), P())
    return jax.shard_map(shards, mesh=mesh, in_specs=in_specs, out_specs=out_specs, check_vma=False)
```

```python
import jax
import jax.numpy as jnp
from jax import lax
from jax.experimental import pallas as pl
from jax.experimental.pallas import tpu as pltpu
from jax.sharding import PartitionSpec as P

EXP, ROWS, FF, R = 2, 192, 8192, 32
REPS, SIDE = 4, 4
UNITS = 4
STREAMS = 6
UNIT = FF // UNITS
PIECE = UNIT // SIDE
TILE = PIECE // SIDE
LANES = 128
LOADS = 4
LOAD = FF // LOADS
MESH = pl.DeviceIdType.MESH
HIGH = lax.Precision.HIGHEST
NN = (((1,), (0,)), ((), ()))
NT = (((1,), (1,)), ((), ()))


def split(value, pieces):
    out = []
    for _ in range(pieces):
        piece = value.astype(jnp.bfloat16)
        out.append(piece)
        value = value - piece.astype(jnp.float32)
    return out


def dot(a, b, dims=NN):
    return lax.dot_general(a, b, dims, preferred_element_type=jnp.float32)


def dot_high(a, b, dims=NN):
    return lax.dot_general(a, b, dims, precision=HIGH, preferred_element_type=jnp.float32)


def kernel(
    g_hbm, e_hbm, q_hbm, fresh, coeffs, g, e, basis,
    q, panels, left, gram1, gram2, aug_ref, part, partner, r1, r1b, s2, r2, t3, full,
    load_sem, ps, pr, g1s, g1r, g2s, g2r, cs, cr, s1s, s1r, s2s, s2r, s3s, s3r, a2s, a2r, a1s, a1r, fs, fr,
):
    y = lax.axis_index("rep")
    row = lax.axis_index("row")
    c = lax.rem(row, 2)
    z = lax.rem(row // 2, SIDE)
    x = row // (2 * SIDE)
    me = (x, y, z)

    def at(place, core):
        return (place[1], place[0] * (2 * SIDE) + place[2] * 2 + core)

    def along(axis, d):
        return at([lax.rem(p + d * w, SIDE) for p, w in zip(me, axis)], c)

    def my(axis):
        return x * axis[0] + y * axis[1] + z * axis[2]

    ax, ay, az = (1, 0, 0), (0, 1, 0), (0, 0, 1)

    def either(first, second, core=c):
        return [tuple(a * (1 - core) + b * core for a, b in zip(p, q)) for p, q in zip(first, second)]

    table = [
        ((ax, ay, az), (ay, az, ax)),
        ((az, ax, ay), (az, ay, ax)),
        ((ay, az, ax), (az, ax, ay)),
        ((ax, ay, az), (ax, az, ay)),
    ]
    orders = [either(*pair) for pair in table]
    orders_there = [either(*pair, 1 - c) for pair in table]
    streams = []
    for j in range(UNITS):
        if j % 2 == 0:
            streams.append((j, pl.ds(0, R), 0, 1))
        else:
            streams.append((j, pl.ds(0, R // 2), 0, 1))
            streams.append((j, pl.ds(R // 2, R // 2), 1, 0))

    def streams_of(ex):
        return [s for s, stream in enumerate(streams) if stream[0] // 2 == ex]

    def axes(s):
        j, _, a, b = streams[s]
        return orders[j][a], orders[j][b]

    def shifted(axis, d):
        return lax.rem(my(axis) + d, SIDE)

    other = at(me, 1 - c)

    def remote(src, dst, send, recv, device):
        return pltpu.make_async_remote_copy(
            src_ref=src, dst_ref=dst, send_sem=send, recv_sem=recv, device_id=device, device_id_type=MESH
        )

    barrier = pltpu.get_barrier_semaphore()
    greeted = [along(axis, d) for axis in (ax, ay, az) for d in (1, 2, 3)]
    greeted += [at((lax.rem(x + d, SIDE), y, z), 1 - c) for d in range(SIDE)]
    for device in greeted:
        pl.semaphore_signal(barrier, inc=1, device_id=device, device_id_type=MESH)

    def loads(ex, h):
        cols = pl.ds(pl.multiple_of(h * LOAD, LOAD), LOAD)
        return [
            pltpu.make_async_copy(q_hbm.at[ex, :, cols], q.at[ex, :, cols], load_sem.at[0, ex, h]),
            pltpu.make_async_copy(g_hbm.at[0, ex, :, cols], g.at[ex, :, cols], load_sem.at[1, ex, h]),
            pltpu.make_async_copy(e_hbm.at[0, ex, :, cols], e.at[ex, :, cols], load_sem.at[2, ex, h]),
        ]

    for ex in range(EXP):
        for h in range(LOADS):
            for copy in loads(ex, h):
                copy.start()

    def to_replica(ex, d):
        spot = panels.at[ex, y]
        return remote(spot, spot, ps.at[ex, d - 1], pr.at[ex, d - 1], along(ay, d))

    def panel_term(ex, _):
        def add(h, total):
            for copy in loads(ex, h):
                copy.wait()
            cols = pl.ds(pl.multiple_of(h * LOAD, LOAD), LOAD)
            q3 = jnp.concatenate(split(q[ex, :, cols], 3), axis=0)
            return total + (dot(g[ex, :, cols], q3, NT) + dot(e[ex, :, cols], q3, NT))

        total = lax.fori_loop(0, LOADS, add, jnp.zeros((ROWS, 3 * R), jnp.float32))
        flat = jnp.concatenate([total, jnp.zeros((ROWS, R), jnp.float32)], axis=1).T
        term = flat[0:R] + flat[R : 2 * R] + flat[2 * R : 3 * R]
        panels[ex, y, 0:R] = term[:, 0:LANES]
        panels[ex, y, R:] = jnp.concatenate([term[: R // 2, LANES:], term[R // 2 :, LANES:]], axis=1)

        @pl.when(ex == 0)
        def _():
            pl.semaphore_wait(barrier, len(greeted))

        for d in (2, 1, 3):
            to_replica(ex, d).start()
        return 0

    lax.fori_loop(0, EXP, panel_term, 0)

    def finish_panel(ex):
        for d in (1, 2, 3):
            to_replica(ex, d).wait_recv()
        packed = (panels[ex, 0] + panels[ex, 1] + panels[ex, 2] + panels[ex, 3]) * (1.0 / REPS)
        rest = packed[R:]
        rest = jnp.concatenate([rest[:, : LANES // 2], rest[:, LANES // 2 :]], axis=0)
        panel = jnp.concatenate([packed[0:R], rest], axis=1)
        left[ex] = jnp.concatenate(split(panel, 3), axis=0)
        return panel

    def unit(j):
        return j // 2, 2 * c + j % 2

    def unit_there(j):
        return j // 2, 2 * (1 - c) + j % 2

    def product(ex, u, p):
        cols = pl.ds(pl.multiple_of(u * UNIT + p * PIECE, PIECE), PIECE)
        both = dot(left[ex], g[ex, :, cols]) + dot(left[ex], e[ex, :, cols])
        part[ex, u, p] = both[0:R] + both[R : 2 * R] + both[2 * R : 3 * R]

    def to_partner(j, p):
        spot = part.at[(*unit_there(j), p)]
        return remote(spot, partner.at[j, p], cs.at[j, p], cr.at[j, p], other)

    def lanes(p):
        return pl.ds(pl.multiple_of(p * TILE, TILE), TILE)

    def scatter1(s, d):
        j, rows, swapped, _ = streams[s]
        axis = axes(s)[0]
        p = shifted(axis, d)
        if swapped:
            src, dst = part.at[(*unit(j), slice(None), rows, lanes(p))], r1b.at[j // 2, d - 1]
        else:
            src, dst = part.at[(*unit(j), p, rows)], r1.at[j, d - 1, rows]
        return remote(src, dst, s1s.at[s, d - 1], s1r.at[s, d - 1], along(axis, d))

    def coefficients(ex):
        units = (2 * ex, 2 * ex + 1)
        for j in units:
            for p in range(SIDE):
                product(*unit_there(j), p)
            for d in (2, 1, 3, 0):
                to_partner(j, shifted(orders_there[j][0], d)).start()
        for j in units:
            for p in range(SIDE):
                product(*unit(j), p)
        for j in units:
            mine = [s for s in streams_of(ex) if streams[s][0] == j]
            for d in (2, 1, 3, 0):
                p = shifted(orders[j][0], d)
                to_partner(j, p).wait_recv()
                spot = (*unit(j), p)
                part[spot] = part[spot] + partner[j, p]
                if d:
                    scatter1(mine[0], d).start()
            for s in mine[1:]:
                for d in (2, 1, 3):
                    scatter1(s, d).start()

    panel0 = finish_panel(0)
    coefficients(0)
    panel1 = finish_panel(1)

    zeros = jnp.zeros((R, ROWS), jnp.float32)
    pad0 = jnp.concatenate([panel0, zeros, zeros, zeros], axis=0)
    pad1 = jnp.concatenate([zeros, zeros, panel1, zeros], axis=0)
    gram1[2 * x + c] = dot_high(panel0, pad0, NT) + dot_high(panel1, pad1, NT)
    gram1_copies = []
    for i in range(7):
        if i < 3:
            device = along(ax, i + 1)
        else:
            device = at((lax.rem(x + i - 3, SIDE), y, z), 1 - c)
        copy = remote(gram1.at[2 * x + c], gram1.at[2 * x + c], g1s.at[i], g1r.at[i], device)
        copy.start()
        gram1_copies.append(copy)

    coefficients(1)

    def scatter2(s, d):
        j, rows, _, _ = streams[s]
        axis = axes(s)[1]
        src, dst = s2.at[j, shifted(axis, d), rows], r2.at[j, d - 1, rows]
        return remote(src, dst, s2s.at[s, d - 1], s2r.at[s, d - 1], along(axis, d))

    def scatter3(j, d):
        axis = orders[j][2]
        i = my(axis)
        return remote(t3.at[j, i], t3.at[j, i], s3s.at[j, d - 1], s3r.at[j, d - 1], along(axis, d))

    def gather2(s, d):
        j, rows, _, _ = streams[s]
        axis = axes(s)[1]
        spot = full.at[(*unit(j), my(orders[j][0]), my(orders[j][1]), rows)]
        return remote(spot, spot, a2s.at[s, d - 1], a2r.at[s, d - 1], along(axis, d))

    def band(s, p):
        j, rows, swapped, _ = streams[s]
        if swapped:
            return full.at[(*unit(j), slice(None), p, rows)]
        return full.at[(*unit(j), p, slice(None), rows)]

    def gather1(s, d):
        axis = axes(s)[0]
        spot = band(s, my(axis))
        return remote(spot, spot, a1s.at[s, d - 1], a1r.at[s, d - 1], along(axis, d))

    def forward(s, d):
        spot = band(s, shifted(axes(s)[0], d))
        return remote(spot, spot, fs.at[s, d], fr.at[s, d], other)

    def exchange2(ex):
        for s in streams_of(ex):
            j, rows, swapped, _ = streams[s]
            for d in (1, 3, 2):
                scatter1(s, d).wait_recv()
            p = my(axes(s)[0])
            if swapped:
                for i in range(SIDE):
                    mine = part[(*unit(j), i, rows, lanes(p))]
                    s2[j, i, rows] = mine + r1b[ex, 0, i] + r1b[ex, 1, i] + r1b[ex, 2, i]
            else:
                mine = part[(*unit(j), p, rows)] + r1[j, 0, rows] + r1[j, 1, rows] + r1[j, 2, rows]
                for i in range(SIDE):
                    s2[j, i, rows] = mine[:, i * TILE : (i + 1) * TILE]
            for d in (2, 1, 3):
                scatter2(s, d).start()

    def exchange3(ex):
        for j in (2 * ex, 2 * ex + 1):
            for s in streams_of(ex):
                if streams[s][0] == j:
                    rows = streams[s][1]
                    for d in (1, 3, 2):
                        scatter2(s, d).wait_recv()
                    mine = s2[j, my(axes(s)[1]), rows]
                    t3[j, my(orders[j][2]), rows] = mine + r2[j, 0, rows] + r2[j, 1, rows] + r2[j, 2, rows]
            for d in (2, 1, 3):
                scatter3(j, d).start()

    def own_tile(ex):
        for j in (2 * ex, 2 * ex + 1):
            for d in (1, 3, 2):
                scatter3(j, d).wait_recv()
            tile = t3[j, 0] + t3[j, 1] + t3[j, 2] + t3[j, 3]
            new = dot_high(aug_ref[ex], jnp.concatenate([tile] * 4, axis=0)) * (1.0 / REPS)
            full[(*unit(j), my(orders[j][0]), my(orders[j][1]))] = new
            for s in streams_of(ex):
                if streams[s][0] == j:
                    for d in (2, 1, 3):
                        gather2(s, d).start()

    def spread(ex):
        for s in streams_of(ex):
            for d in (1, 3, 2):
                gather2(s, d).wait_recv()
            for d in (2, 1, 3):
                gather1(s, d).start()
            forward(s, 0).start()

    exchange2(0)
    for copy in gram1_copies:
        copy.wait_recv()
    total = gram1[0]
    for i in range(1, 2 * SIDE):
        total += gram1[i]
    gram2[z] = total
    gram2_copies = []
    for d in (2, 1, 3):
        copy = remote(gram2.at[z], gram2.at[z], g2s.at[d - 1], g2r.at[d - 1], along(az, d))
        copy.start()
        gram2_copies.append(copy)

    exchange2(1)
    exchange3(0)

    exchange3(1)

    for copy in gram2_copies:
        copy.wait_recv()
    aug = gram2[0] + gram2[1] + gram2[2] + gram2[3]
    rows_at = lax.broadcasted_iota(jnp.int32, (R, 4 * R), 0)
    lanes_at = lax.broadcasted_iota(jnp.int32, (R, 4 * R), 1)
    unit_at = (lanes_at == rows_at + R) | (lanes_at == rows_at + 3 * R)
    aug = jnp.where(unit_at, 1.0, aug)
    first = lanes_at < 2 * R
    pivots = jnp.ones((R, 4 * R), jnp.float32)
    for k in range(0, R, 2):
        col = [jnp.where(first, aug[:, i : i + 1], aug[:, 2 * R + i : 2 * R + i + 1]) for i in (k, k + 1)]
        row = [aug[i : i + 1, :] for i in (k, k + 1)]
        top, side, low = col[0][k : k + 1, :], col[0][k + 1 : k + 2, :], col[1][k + 1 : k + 2, :]
        scale = side / top
        ratio = row[0] / top
        below = row[1] - scale * row[0]
        pivot = low - scale * side
        col[1] = col[1] - col[0] * scale
        pivots = jnp.where(rows_at == k, top, jnp.where(rows_at == k + 1, pivot, pivots))
        rest = aug - col[0] * ratio - col[1] * (below / pivot)
        aug = jnp.where(rows_at > k + 1, rest, jnp.where(rows_at == k + 1, below, aug))
    aug = aug / jnp.sqrt(pivots)
    for ex in range(EXP):
        wanted = (lanes_at >= (2 * ex + 1) * R) & (lanes_at < (2 * ex + 2) * R)
        aug_ref[ex] = jnp.where(wanted, aug, 0.0)

    own_tile(0)

    own_tile(1)
    for ex, panel in ((0, panel0), (1, panel1)):
        b = dot_high(aug_ref[ex], jnp.concatenate([panel] * 4, axis=0))
        hi, lo = [piece.astype(jnp.float32) for piece in split(b, 2)]
        basis[ex] = jnp.concatenate([hi, hi, lo, lo], axis=0).T.astype(jnp.bfloat16)

    spread(0)
    spread(1)

    for ex in range(EXP):
        for d in (1, 2, 3):
            to_replica(ex, d).wait_send()
    for copy in gram1_copies + gram2_copies:
        copy.wait_send()
    for j in range(UNITS):
        for d in range(SIDE):
            to_partner(j, d).wait_send()
        for d in (1, 2, 3):
            scatter3(j, d).wait_send()
    for s in range(len(streams)):
        for d in (1, 2, 3):
            for copy in (scatter1(s, d), scatter2(s, d)):
                copy.wait_send()

    def finish_unit(ex, u, errors):
        for p in range(SIDE):
            cols = pl.ds(pl.multiple_of(u * UNIT + p * PIECE, PIECE), PIECE)
            coeffs[ex, :, cols] = jnp.concatenate([full[ex, u, p, i] for i in range(SIDE)], axis=1)
            if errors:
                fresh[:, cols] = residual(g, e, basis, coeffs, ex, cols)

    for ex in range(EXP):
        for j in (2 * ex, 2 * ex + 1):
            for s in streams_of(ex):
                if streams[s][0] == j:
                    for d in (1, 3, 2):
                        gather1(s, d).wait_recv()
                        forward(s, SIDE - d).start()
            finish_unit(*unit(j), ex == 0)
    for s in range(len(streams)):
        for d in (1, 2, 3):
            for copy in (gather2(s, d), gather1(s, d)):
                copy.wait_send()
    for j in range(UNITS):
        for s in streams_of(j // 2):
            if streams[s][0] == j:
                for d in range(SIDE):
                    forward(s, d).wait_recv()
        finish_unit(*unit_there(j), j < 2)

    for s in range(len(streams)):
        for d in range(SIDE):
            forward(s, d).wait_send()


def residual(g, e, basis, coeffs, ex, cols):
    hi, lo = split(coeffs[ex, :, cols], 2)
    low = dot(basis[ex], jnp.concatenate([hi, lo, hi, lo], axis=0))
    merged = g[ex, :, cols].astype(jnp.float32) + e[ex, :, cols].astype(jnp.float32)
    return (merged - low).astype(jnp.bfloat16)


def store(fresh0, coeffs, g, e, basis, fresh_out, coeffs_out, fresh1, sem):
    copies = []

    def send(src, dst):
        copies.append(pltpu.make_async_copy(src, dst, sem.at[len(copies)]))
        copies[-1].start()

    units = [pl.ds(u * UNIT, UNIT) for u in range(UNITS)]
    for cols in units:
        send(fresh0.at[:, cols], fresh_out.at[0, 0, :, cols])
    for ex in range(EXP):
        send(coeffs.at[ex], coeffs_out.at[ex])
    for u in range(UNITS):
        for p in range(SIDE):
            cols = pl.ds(u * UNIT + p * PIECE, PIECE)
            fresh1[:, cols] = residual(g, e, basis, coeffs, 1, cols)
        send(fresh1.at[:, units[u]], fresh_out.at[0, 1, :, units[u]])
    for copy in copies:
        copy.wait()


def shards(grads, errors, q_init):
    dma = pltpu.SemaphoreType.DMA
    anywhere = pl.BlockSpec(memory_space=pl.ANY)
    vmem = pl.BlockSpec(memory_space=pltpu.VMEM)
    f32, b16 = jnp.float32, jnp.bfloat16
    held = pl.pallas_call(
        kernel,
        out_shape=(
            pltpu.VMEM((ROWS, FF), b16),
            pltpu.VMEM((EXP, R, FF), f32),
            pltpu.VMEM((EXP, ROWS, FF), b16),
            pltpu.VMEM((EXP, ROWS, FF), b16),
            pltpu.VMEM((EXP, ROWS, 4 * R), b16),
        ),
        in_specs=[anywhere] * 3,
        out_specs=(vmem,) * 5,
        scratch_shapes=[
            pltpu.VMEM((EXP, R, FF), f32),
            pltpu.VMEM((EXP, REPS, R + R // 2, LANES), f32),
            pltpu.VMEM((EXP, 3 * R, ROWS), b16),
            pltpu.VMEM((2 * SIDE, R, 4 * R), f32),
            pltpu.VMEM((SIDE, R, 4 * R), f32),
            pltpu.VMEM((EXP, R, 4 * R), f32),
            pltpu.VMEM((EXP, UNITS, SIDE, R, PIECE), f32),
            pltpu.VMEM((UNITS, SIDE, R, PIECE), f32),
            pltpu.VMEM((UNITS, SIDE - 1, R, PIECE), f32),
            pltpu.VMEM((EXP, SIDE - 1, SIDE, R // 2, TILE), f32),
            pltpu.VMEM((UNITS, SIDE, R, TILE), f32),
            pltpu.VMEM((UNITS, SIDE - 1, R, TILE), f32),
            pltpu.VMEM((UNITS, SIDE, R, TILE), f32),
            pltpu.VMEM((EXP, UNITS, SIDE, SIDE, R, TILE), f32),
            dma((3, EXP, LOADS)),
            dma((EXP, 3)), dma((EXP, 3)),
            dma((7,)), dma((7,)), dma((3,)), dma((3,)),
            dma((UNITS, SIDE)), dma((UNITS, SIDE)),
            dma((STREAMS, 3)), dma((STREAMS, 3)),
            dma((STREAMS, 3)), dma((STREAMS, 3)),
            dma((UNITS, 3)), dma((UNITS, 3)),
            dma((STREAMS, 3)), dma((STREAMS, 3)),
            dma((STREAMS, 3)), dma((STREAMS, 3)),
            dma((STREAMS, SIDE)), dma((STREAMS, SIDE)),
        ],
        compiler_params=pltpu.CompilerParams(
            collective_id=0, has_side_effects=True, vmem_limit_bytes=44 * 2**20
        ),
        cost_estimate=pl.CostEstimate(flops=10**9, bytes_accessed=25 * 10**6, transcendentals=0),
        name="compress",
    )(grads, errors, q_init)
    return pl.pallas_call(
        store,
        out_shape=(
            jax.ShapeDtypeStruct((1, EXP, ROWS, FF), b16),
            jax.ShapeDtypeStruct((EXP, R, FF), f32),
        ),
        in_specs=[anywhere] + [vmem] * 4,
        out_specs=(anywhere, anywhere),
        scratch_shapes=[pltpu.VMEM((ROWS, FF), b16), dma((2 * UNITS + EXP,))],
        compiler_params=pltpu.CompilerParams(has_side_effects=True, vmem_limit_bytes=8 * 2**20),
        name="store",
    )(*held)


def solution(mesh):
    in_specs = (P("rep", None, "row", None), P("rep", None, "row", None), P())
    out_specs = (P("rep", None, "row", None), P())
    return jax.shard_map(shards, mesh=mesh, in_specs=in_specs, out_specs=out_specs, check_vma=False)
```
